32 devices in a mesh: parts: 2 (over x), dp: 16 (over z, y, core).
Axes of the slice: x: 2, y: 2, z: 4, core: 2. Of those that a mesh axis runs over, the one named last changes fastest.
Arguments:
- hidden_rows: bfloat16 [4096, 4096], P(('parts', 'dp')), parts along dimension 0, may hold values from -6 to 6
- queries: bfloat16 [4096, 4096], P(('parts', 'dp')), parts along dimension 0, may hold values from -0.5390625 to 0.5390625
- keys: bfloat16 [4096, 512], P(('parts', 'dp')), parts along dimension 0, may hold values from -6 to 6
- down_basis: bfloat16 [8192, 512], P('parts'), parts along dimension 0, may hold values from -0.09375 to 0.09375
- up_basis: bfloat16 [8, 128, 128], P('parts'), parts along dimension 0, may hold values from -0.5 to 0.5
- head_group: int32 [32], replicated, may hold values from 0 to 3, as said below
Outputs:
- down_new: bfloat16 [8192, 512], P(('parts', 'dp')), parts along dimension 0
- up_new: bfloat16 [8, 128, 128], P('parts'), parts along dimension 0
- row_error: float32 [4096], P(('parts', 'dp')), parts along dimension 0
The draws below stay inside these ranges and needn't reach their ends.
There are 2 independent parts, one for each index of `parts`. The reference program is written for one: setup_inputs(seed, part) draws one part's arguments, and reference() takes and returns one part's arrays. A program takes and returns all parts, laid end to end along the dimension named above; an argument that names none is the same for every part. Nothing has to cross between parts.
Inputs may be any that keep to these rules, and one draw needn't show every extreme that they name: `head_group`: each of the 4 groups holds exactly 8 heads.
All inputs are finite; a program needn't handle non-finite values.
Results may differ from the reference program's by a relative error of at most 0.006.
Values may be sent and summed in bfloat16 or wider, within the bound.
A program may use at most 128 MiB of HBM per device.

```python
import math
import jax
import jax.numpy as jnp
from jax import lax

D = 4096
HEADS = 32
GROUPS = 4
HD = 128
TOK_DEV = 128
TOKENS = 2048


def draw_head_group(key, part):
    key = jax.random.fold_in(key, 7)
    order = jax.random.permutation(key, HEADS)
    return (order % GROUPS).astype(jnp.int32)


def block_levels(key, extent, shards, smallest, high):
    def one(dim, parts):
        draws = jax.random.uniform(jax.random.fold_in(jax.random.fold_in(key, 6), dim), (parts,), jnp.float32, smallest / len(shards), high / len(shards))
        return jnp.repeat(jnp.exp(draws), extent[dim] // parts).reshape((-1,) + (1,) * (len(extent) - dim - 1))

    level = one(*shards[0])
    for cut in shards[1:]:
        level = level * one(*cut)
    return level


def bell_draw(own_key, dims, spread, most, cuts=(), kind=jnp.bfloat16):
    loudness = block_levels(own_key, dims, cuts, -0.22, 0.18) if cuts else 1.0
    entries = jax.random.normal(own_key, dims, jnp.float32) * spread * loudness
    return jnp.minimum(jnp.maximum(entries, -most), most).astype(kind)


def setup_inputs(seed: int = 0, part: int = 0) -> dict:
    seeds = jax.random.split(jax.random.key(seed), 7)
    part_splits = jax.random.split(jax.random.fold_in(seeds[6], part), 7)
    return {
        "hidden_rows": bell_draw(part_splits[0], (TOKENS, D), 1.0, 6.0, ((0, 16),)),
        "queries": bell_draw(part_splits[1], (TOKENS, HEADS * HD), 0.09, 0.5390625, ((0, 16),)),
        "keys": bell_draw(part_splits[2], (TOKENS, GROUPS * HD), 1.0, 6.0, ((0, 16),)),
        "down_basis": bell_draw(part_splits[3], (D, GROUPS * HD), D ** -0.5, 0.09375),
        "up_basis": bell_draw(part_splits[4], (GROUPS, HD, HD), HD ** -0.5, 0.5),
        "head_group": draw_head_group(jax.random.fold_in(seeds[6], 71), part),
    }


PRECISE = lax.Precision.HIGHEST
RATE_DOWN = 1.0
RATE_UP = 8.0

def reference(hidden_rows, queries, keys, down_basis, up_basis, head_group):
    select_f = (head_group[:, None] == jnp.arange(GROUPS, dtype=jnp.int32)[None, :]).astype(jnp.float32)
    block_count = TOKENS // TOK_DEV
    q_blocks = queries.reshape(block_count, TOK_DEV, HEADS, HD)
    causal = jnp.arange(TOK_DEV)[:, None] >= jnp.arange(TOK_DEV)[None, :]
    pair_scale = 2.0 / (TOKENS * TOKENS * HEADS)
    root_tokens = math.sqrt(TOKENS)
    zero_gram = jnp.zeros((GROUPS, HD, HD), jnp.float32)

    def forward(down, up):
        latent = jnp.dot(hidden_rows, down, preferred_element_type=jnp.float32).astype(jnp.bfloat16)
        recon = jnp.einsum('ngd,gde->nge', latent.reshape(TOKENS, GROUPS, HD).astype(jnp.float32), up.astype(jnp.float32), precision=PRECISE)
        err_rows = (keys.reshape(TOKENS, GROUPS, HD).astype(jnp.float32) - recon).astype(jnp.bfloat16)
        return (latent, err_rows)

    def local_scores(q_block, e_block):
        q_wide = q_block.astype(jnp.float32)
        e_heads = jnp.einsum('jgd,hg->jhd', e_block.astype(jnp.float32), select_f, precision=PRECISE)
        scores = jnp.einsum('ihd,jhd->hij', q_wide, e_heads, precision=PRECISE)
        return jnp.where(causal[None], scores, 0.0)

    def gradient(err_rows):
        e_blocks = err_rows.reshape(block_count, TOK_DEV, GROUPS, HD)

        def advance(tail_gram, blocks_in):
            q_block, e_block = blocks_in
            q_wide = q_block.astype(jnp.float32)
            scores_b = local_scores(q_block, e_block).astype(jnp.bfloat16).astype(jnp.float32)
            local_part = jnp.einsum('hij,ihd->jhd', scores_b, q_wide, precision=PRECISE)
            local_groups = jnp.einsum('jhd,hg->jgd', local_part, select_f, precision=PRECISE)
            cross_part = jnp.einsum('jgd,gde->jge', e_block.astype(jnp.float32), tail_gram, precision=PRECISE)
            head_gram = jnp.einsum('ihd,ihe->hde', q_wide, q_wide, precision=PRECISE)
            q_gram = jnp.einsum('hde,hg->gde', head_gram, select_f, precision=PRECISE)
            return (tail_gram + q_gram, pair_scale * (local_groups + cross_part))
        unused, grad_blocks = lax.scan(advance, zero_gram, (q_blocks, e_blocks), reverse=True)
        return grad_blocks.reshape(TOKENS, GROUPS, HD).astype(jnp.bfloat16)

    def update(down, up, latent, grad_errs):
        latent_grad = (-jnp.einsum('jge,gde->jgd', grad_errs.astype(jnp.float32), up.astype(jnp.float32), precision=PRECISE)).astype(jnp.bfloat16).reshape(TOKENS, GROUPS * HD)
        down_grad = lax.dot_general(hidden_rows, latent_grad, (((0,), (0,)), ((), ())), preferred_element_type=jnp.float32)
        up_grad = -jnp.einsum('jgd,jge->gde', latent.reshape(TOKENS, GROUPS, HD).astype(jnp.float32), grad_errs.astype(jnp.float32), precision=PRECISE)
        new_down = (down.astype(jnp.float32) - RATE_DOWN * root_tokens * down_grad).astype(jnp.bfloat16)
        new_up = (up.astype(jnp.float32) - RATE_UP * root_tokens * up_grad).astype(jnp.bfloat16)
        return (new_down, new_up)

    def row_errors(err_rows):
        e_blocks = err_rows.reshape(block_count, TOK_DEV, GROUPS, HD)

        def advance(prefix, blocks_in):
            q_block, e_block = blocks_in
            q_wide = q_block.astype(jnp.float32)
            scores = local_scores(q_block, e_block)
            local_part = lax.optimization_barrier(jnp.sum(scores * scores, axis=(0, 2)))
            p_heads = jnp.einsum('hg,gde->hde', select_f, prefix, precision=PRECISE)
            q_moved = jnp.einsum('ihd,hde->ihe', q_wide, p_heads, precision=PRECISE)
            remote = lax.optimization_barrier(jnp.sum(q_moved * q_wide, axis=(1, 2)))
            e_wide = e_block.astype(jnp.float32)
            key_gram = jnp.einsum('jgd,jge->gde', e_wide, e_wide, precision=PRECISE)
            return (prefix + key_gram, remote + local_part)
        unused, totals = lax.scan(advance, zero_gram, (q_blocks, e_blocks))
        totals = totals.reshape(TOKENS)
        return totals / ((jnp.arange(TOKENS) + 1).astype(jnp.float32) * HEADS)
    latent, err_rows = forward(down_basis, up_basis)
    down_one, up_one = update(down_basis, up_basis, latent, gradient(err_rows))
    latent, err_rows = forward(down_one, up_one)
    row_error = row_errors(err_rows)
    down_two, up_two = update(down_one, up_one, latent, gradient(err_rows))
    return (down_two, up_two, row_error)
```

```python
import functools
import math

import jax
import jax.numpy as jnp
from jax import lax
from jax.experimental import pallas as pl
from jax.experimental.pallas import tpu as pltpu
from jax.sharding import PartitionSpec as P

HEADS = 32
GROUPS = 4
HD = 128
PER = HEADS // GROUPS
WIDTH = GROUPS * HD
RATE_DOWN = 1.0
RATE_UP = 8.0
F32 = jnp.float32
BF16 = jnp.bfloat16
MESH = pl.DeviceIdType.MESH


def mm(a, b, dims=((1,), (0,))):
    return lax.dot_general(a, b, (dims, ((), ())), preferred_element_type=F32)


def split(x):
    hi = x.astype(BF16)
    return hi, (x - hi.astype(F32)).astype(BF16)


def sort_heads(order, queries, qs):
    tok = queries.shape[0]
    for s in range(HEADS):
        col = pl.multiple_of(order[s] * HD, HD)
        qs[s * tok:(s + 1) * tok] = queries[:, pl.ds(col, HD)]


def kernel(
    n, tok, feat,
    hid, qs, keys, down0, up0,
    rows_out, up_out, err_out,
    hid_t, feats, latent_b, gl1, gl2, down1, gram, kgram, upl1, upl2,
    stages, results, finals,
    a2a_s, a2a_r, p1_s, p1_r, p2_s, p2_r, agz_s, agy_s, agc_s, ag_r,
):
    me = lax.axis_index("dp")
    planes = n // 4
    zi, yi, ci = me // 4, (me // 2) % 2, me % 2
    ypeer = zi * 4 + (1 - yi) * 2 + ci
    cpeer = zi * 4 + yi * 2 + (1 - ci)
    part = feat // n
    piece = WIDTH // n
    total = n * tok
    pair_scale = 2.0 / (total * total * HEADS)
    root = math.sqrt(total)

    def remote(src, dst, s, r, to):
        return pltpu.make_async_remote_copy(
            src_ref=src, dst_ref=dst, send_sem=s, recv_sem=r,
            device_id={"dp": to}, device_id_type=MESH,
        )

    def peers(body):
        def one(k, carry):
            body(lax.rem(me + k, n))
            return carry

        lax.fori_loop(1, n, one, 0)

    def phase1_desc(u, src, owner, to):
        return remote(
            src.at[pl.ds(pl.multiple_of(to * piece, piece), piece)],
            stages.at[u, owner], p1_s.at[u, to], p1_r.at[u, owner], to,
        )

    def phase1_start(u, src):
        peers(lambda p: phase1_desc(u, src, me, p).start())
        stages[u, me] = src[pl.ds(pl.multiple_of(me * piece, piece), piece)]

    def phase2_desc(u, owner, to):
        return remote(
            results.at[u, to],
            finals.at[u, pl.ds(pl.multiple_of(owner * piece, piece), piece)],
            p2_s.at[u, to], p2_r.at[u, owner], to,
        )

    def phase2_start(u, src, mode):
        peers(lambda p: phase1_desc(u, src, p, p).wait_recv())
        zero = jnp.zeros((piece, HD), F32)
        if mode == "sum":
            tot = lax.fori_loop(0, n, lambda k, a: a + stages[u, k], zero)

            def put(k, carry):
                results[u, k] = tot
                return carry

            lax.fori_loop(0, n, put, 0)
        else:
            def scan(k, a):
                at = n - 1 - k if mode == "suffix" else k
                results[u, at] = a
                return a + stages[u, at]

            lax.fori_loop(0, n, scan, zero)
        peers(lambda p: phase2_desc(u, me, p).start())
        finals[u, pl.ds(pl.multiple_of(me * piece, piece), piece)] = results[u, me]

    def phase2_wait(u):
        peers(lambda p: phase2_desc(u, p, p).wait_recv())

    def exchange_sends_done(u, src):
        peers(lambda p: phase1_desc(u, src, me, p).wait_send())
        peers(lambda p: phase2_desc(u, me, p).wait_send())

    def blk(buf, rows, b):
        return buf.at[pl.ds(pl.multiple_of(b * rows, rows), rows)]

    def ag_desc(u, buf, rows, b, to, sem):
        ref = blk(buf, rows, b)
        return remote(ref, ref, sem, ag_r.at[u, b], to)

    def zblock(k):
        return lax.rem(zi + k, planes) * 4 + yi * 2 + ci

    def yblock(k):
        return lax.rem(zi + k, planes) * 4 + (1 - yi) * 2 + ci

    def gather(u, buf, rows):
        def loop(lo, hi, body):
            def one(k, carry):
                body(k)
                return carry

            lax.fori_loop(lo, hi, one, 0)

        def arrived(b):
            ag_desc(u, buf, rows, b, b, agy_s.at[u, b]).wait_recv()

        def to_z(k):
            ag_desc(u, buf, rows, me, zblock(k), agz_s.at[u, k]).start()

        def to_y(b):
            ag_desc(u, buf, rows, b, ypeer, agy_s.at[u, b]).start()

        def to_c(b):
            ag_desc(u, buf, rows, b, cpeer, agc_s.at[u, b]).start()

        loop(1, planes, to_z)
        to_y(me)
        to_c(me)

        def from_z(k):
            b = zblock(k)
            arrived(b)
            to_y(b)
            to_c(b)

        loop(1, planes, from_z)

        def from_y(k):
            b = yblock(k)
            arrived(b)
            to_c(b)

        loop(0, planes, from_y)

        def from_c(k):
            arrived(lax.rem(zi + k // 2, planes) * 4 + lax.rem(k, 2) * 2 + (1 - ci))

        loop(0, 2 * planes, from_c)

    def gather_sends_done(u, buf, rows):
        def z(k, carry):
            ag_desc(u, buf, rows, me, zblock(k), agz_s.at[u, k]).wait_send()
            return carry

        lax.fori_loop(1, planes, z, 0)

        def yc(k, carry):
            b = zblock(k)
            ag_desc(u, buf, rows, b, ypeer, agy_s.at[u, b]).wait_send()
            ag_desc(u, buf, rows, b, cpeer, agc_s.at[u, b]).wait_send()
            b = yblock(k)
            ag_desc(u, buf, rows, b, cpeer, agc_s.at[u, b]).wait_send()
            return carry

        lax.fori_loop(0, planes, yc, 0)

    def a2a_desc(owner, to):
        return remote(
            hid_t.at[pl.ds(pl.multiple_of(to * part, part), part)],
            feats.at[:, pl.ds(pl.multiple_of(owner * tok, tok), tok)],
            a2a_s.at[to], a2a_r.at[owner], to,
        )

    barrier = pltpu.get_barrier_semaphore()
    peers(lambda p: pl.semaphore_signal(barrier, inc=1, device_id={"dp": p}, device_id_type=MESH))

    span = PER * tok

    def group_q(g):
        return qs[g * span:(g + 1) * span]

    for g in range(GROUPS):
        q = group_q(g)
        gram[g * HD:(g + 1) * HD] = mm(q, q, ((0,), (0,)))

    pl.semaphore_wait(barrier, n - 1)
    phase1_start(0, gram)

    def turn(k, carry):
        at = pl.multiple_of(k * HD, HD)
        hid_t[pl.ds(at, HD)] = hid[:, pl.ds(at, HD)].T
        return carry

    lax.fori_loop(0, feat // HD, turn, 0)
    peers(lambda p: a2a_desc(me, p).start())
    feats[:, pl.ds(pl.multiple_of(me * tok, tok), tok)] = hid_t[
        pl.ds(pl.multiple_of(me * part, part), part)
    ]

    row = lax.rem(lax.broadcasted_iota(jnp.int32, (span, tok), 0), tok)
    causal = row >= lax.broadcasted_iota(jnp.int32, (span, tok), 1)

    def forward(down, ups):
        step = min(1024, feat)

        def one(k, acc):
            at = pl.multiple_of(k * step, step)
            return acc + mm(hid[:, pl.ds(at, step)], down[pl.ds(at, step)])

        acc = lax.fori_loop(0, feat // step, one, jnp.zeros((tok, WIDTH), F32))
        latent_b[...] = acc.astype(BF16)
        errs = []
        for g in range(GROUPS):
            cols = slice(g * HD, (g + 1) * HD)
            recon = mm(latent_b[:, cols], ups[g])
            errs.append((keys[:, cols].astype(F32) - recon).astype(BF16))
        return errs

    def local_scores(errs, g):
        s = mm(group_q(g), errs[g], ((1,), (1,)))
        return jnp.where(causal, s, 0.0)

    def errors_grad(g, errs, local):
        hi, lo = split(finals[0, g * HD:(g + 1) * HD])
        cross = mm(errs[g], hi) + mm(errs[g], lo)
        return (pair_scale * (local + cross)).astype(BF16)

    def gradients(errs, locals_, ups, gl, upl):
        for g in range(GROUPS):
            cols = slice(g * HD, (g + 1) * HD)
            ge = errors_grad(g, errs, locals_[g])
            lg = (-mm(ge, ups[g], ((1,), (1,)))).astype(BF16)
            gl[pl.ds(pl.multiple_of(me * tok, tok), tok), cols] = lg
            upl[cols] = -mm(latent_b[:, cols], ge, ((0,), (0,)))

    def new_rows(old, gl):
        step = 1024

        def one(k, acc):
            at = pl.multiple_of(k * step, step)
            return acc + mm(feats[:, pl.ds(at, step)], gl[pl.ds(at, step)])

        acc = lax.fori_loop(0, total // step, one, jnp.zeros((part, WIDTH), F32))
        return (old.astype(F32) - RATE_DOWN * root * acc).astype(BF16)

    def new_up(old, u, g):
        grad = finals[u, g * HD:(g + 1) * HD]
        return (old.astype(F32) - RATE_UP * root * grad).astype(BF16)

    mine = pl.ds(pl.multiple_of(me * part, part), part)

    ups = [up0[g] for g in range(GROUPS)]
    errs = forward(down0, ups)
    phase2_start(0, gram, "suffix")
    locals_ = []
    for g in range(GROUPS):
        s = local_scores(errs, g).astype(BF16)
        locals_.append(mm(s, group_q(g), ((0,), (0,))))
    phase2_wait(0)
    gradients(errs, locals_, ups, gl1, upl1)
    phase1_start(1, upl1)
    gather(0, gl1, tok)
    peers(lambda p: a2a_desc(p, p).wait_recv())
    phase2_start(1, upl1, "sum")
    down1[mine] = new_rows(down0[mine], gl1)
    gather(1, down1, part)
    phase2_wait(1)

    ups = [new_up(up0[g], 1, g) for g in range(GROUPS)]
    errs = forward(down1, ups)
    for g in range(GROUPS):
        kgram[g * HD:(g + 1) * HD] = mm(errs[g], errs[g], ((0,), (0,)))
    phase1_start(2, kgram)
    locals_ = []
    sums = jnp.zeros((tok, 1), F32)
    for g in range(GROUPS):
        s = local_scores(errs, g)
        own = jnp.sum(s * s, axis=1, keepdims=True)
        for h in range(PER):
            sums = sums + own[h * tok:(h + 1) * tok]
        locals_.append(mm(s.astype(BF16), group_q(g), ((0,), (0,))))
    gradients(errs, locals_, ups, gl2, upl2)
    phase1_start(3, upl2)
    phase2_start(2, kgram, "prefix")
    gather(2, gl2, tok)
    phase2_start(3, upl2, "sum")
    rows_out[...] = new_rows(down1[mine], gl2)
    phase2_wait(2)
    for g in range(GROUPS):
        q = group_q(g)
        hi, lo = split(finals[2, g * HD:(g + 1) * HD])
        moved = mm(q, hi) + mm(q, lo)
        far = jnp.sum(moved * q.astype(F32), axis=1, keepdims=True)
        for h in range(PER):
            sums = sums + far[h * tok:(h + 1) * tok]
    where = (me * tok + 1 + lax.broadcasted_iota(jnp.int32, (tok, 1), 0)).astype(F32)
    err_out[...] = sums / (where * HEADS)
    phase2_wait(3)
    for g in range(GROUPS):
        up_out[g] = new_up(ups[g], 3, g)

    peers(lambda p: a2a_desc(me, p).wait_send())
    exchange_sends_done(0, gram)
    exchange_sends_done(1, upl1)
    exchange_sends_done(2, kgram)
    exchange_sends_done(3, upl2)
    gather_sends_done(0, gl1, tok)
    gather_sends_done(1, down1, part)
    gather_sends_done(2, gl2, tok)


def shards(hidden_rows, queries, keys, down_basis, up_basis, head_group):
    tok, feat = hidden_rows.shape
    n = lax.axis_size("dp")
    part = feat // n
    piece = WIDTH // n
    heads = jnp.arange(HEADS, dtype=jnp.int32)
    same = head_group[:, None] == head_group[None, :]
    before = jnp.sum((same & (heads[None, :] < heads[:, None])).astype(jnp.int32), axis=1)
    place = head_group * PER + before
    order = jnp.sum(jnp.where(place[None, :] == heads[:, None], heads[None, :], 0), axis=1)
    vmem = pl.BlockSpec(memory_space=pltpu.VMEM)
    dma = pltpu.SemaphoreType.DMA
    qs = pl.pallas_call(
        sort_heads,
        out_shape=jax.ShapeDtypeStruct((HEADS * tok, HD), BF16),
        in_specs=[pl.BlockSpec(memory_space=pltpu.SMEM), vmem],
        out_specs=vmem,
    )(order, queries)
    rows, up, err = pl.pallas_call(
        functools.partial(kernel, n, tok, feat),
        out_shape=(
            jax.ShapeDtypeStruct((part, WIDTH), BF16),
            jax.ShapeDtypeStruct((GROUPS, HD, HD), BF16),
            jax.ShapeDtypeStruct((tok, 1), F32),
        ),
        in_specs=[vmem] * 5,
        out_specs=(vmem, vmem, vmem),
        scratch_shapes=[
            pltpu.VMEM((feat, tok), BF16),
            pltpu.VMEM((part, n * tok), BF16),
            pltpu.VMEM((tok, WIDTH), BF16),
            pltpu.VMEM((n * tok, WIDTH), BF16),
            pltpu.VMEM((n * tok, WIDTH), BF16),
            pltpu.VMEM((feat, WIDTH), BF16),
            pltpu.VMEM((WIDTH, HD), F32),
            pltpu.VMEM((WIDTH, HD), F32),
            pltpu.VMEM((WIDTH, HD), F32),
            pltpu.VMEM((WIDTH, HD), F32),
            pltpu.VMEM((4, n, piece, HD), F32),
            pltpu.VMEM((4, n, piece, HD), F32),
            pltpu.VMEM((4, WIDTH, HD), F32),
            dma((n,)), dma((n,)),
            dma((4, n)), dma((4, n)), dma((4, n)), dma((4, n)),
            dma((3, n // 4)), dma((3, n)), dma((3, n)), dma((3, n)),
        ],
        compiler_params=pltpu.CompilerParams(
            collective_id=0, has_side_effects=True, vmem_limit_bytes=48 * 1024 * 1024
        ),
    )(hidden_rows, qs, keys, down_basis, up_basis)
    return rows, up, err.reshape(tok)


def solution(mesh):
    return jax.shard_map(
        shards,
        mesh=mesh,
        in_specs=(
            P(("parts", "dp"), None),
            P(("parts", "dp"), None),
            P(("parts", "dp"), None),
            P("parts", None),
            P("parts", None, None),
            P(),
        ),
        out_specs=(P(("parts", "dp"), None), P("parts", None, None), P(("parts", "dp"))),
        check_vma=False,
    )
```

```python
import functools
import math

import jax
import jax.numpy as jnp
from jax import lax
from jax.experimental import pallas as pl
from jax.experimental.pallas import tpu as pltpu
from jax.sharding import PartitionSpec as P

HEADS = 32
GROUPS = 4
HD = 128
PER = HEADS // GROUPS
WIDTH = GROUPS * HD
CHUNK = 64
RATE_DOWN = 1.0
RATE_UP = 8.0
F32 = jnp.float32
BF16 = jnp.bfloat16
MESH = pl.DeviceIdType.MESH


def mm(a, b, dims=((1,), (0,))):
    return lax.dot_general(a, b, (dims, ((), ())), preferred_element_type=F32)


def sort_heads(order, queries, qs):
    tok = queries.shape[0]
    for s in range(HEADS):
        col = pl.multiple_of(order[s] * HD, HD)
        qs[s * tok:(s + 1) * tok] = queries[:, pl.ds(col, HD)]


def kernel(
    n, tok, feat,
    hid, qs, keys, down0, up0,
    rows_out, up_out, err_out,
    hid_t, feats, latent_b, gl1, gl2, down1, gram, kgram, upl1, upl2,
    stages, results, finals,
    a2a_s, a2a_r, p1_s, p1_r, p2_s, p2_r, agz_s, agy_s, agc_s, agc_r, ag_r,
):
    me = lax.axis_index("dp")
    planes = n // 4
    zi, yi, ci = me // 4, lax.rem(me // 2, 2), lax.rem(me, 2)
    ypeer = zi * 4 + (1 - yi) * 2 + ci
    cpeer = zi * 4 + yi * 2 + (1 - ci)
    part = feat // n
    owners = min(n, WIDTH // 16)
    piece = WIDTH // owners
    total = n * tok
    pair_scale = 2.0 / (total * total * HEADS)
    root = math.sqrt(total)

    def remote(src, dst, s, r, to):
        return pltpu.make_async_remote_copy(
            src_ref=src, dst_ref=dst, send_sem=s, recv_sem=r,
            device_id={"dp": to}, device_id_type=MESH,
        )

    def many(ref, sem):
        return remote(ref, ref, sem, sem, cpeer)

    def peers(body):
        def one(k, carry):
            body(lax.rem(me + k, n))
            return carry

        lax.fori_loop(1, n, one, 0)

    def owning(p, body):
        if owners == n:
            body()
        else:
            pl.when(p < owners)(body)

    def phase1_desc(u, src, owner, to):
        return remote(
            src.at[pl.ds(pl.multiple_of(to * piece, piece), piece)],
            stages.at[u, owner], p1_s.at[u], p1_r.at[u], to,
        )

    def phase1_start(u, src):
        peers(lambda p: owning(p, lambda: phase1_desc(u, src, me, p).start()))

        def keep():
            stages[u, me] = src[pl.ds(pl.multiple_of(me * piece, piece), piece)]

        owning(me, keep)

    def phase2_desc(u, owner, to):
        return remote(
            results.at[u, to],
            finals.at[u, pl.ds(pl.multiple_of(owner * piece, piece), piece)],
            p2_s.at[u], p2_r.at[u], to,
        )

    def phase2_start(u, src, mode):
        def own():
            many(stages.at[u, pl.ds(0, n - 1)], p1_r.at[u]).wait_recv()
            zero = jnp.zeros((piece, HD), F32)
            if mode == "sum":
                tot = lax.fori_loop(0, n, lambda k, a: a + stages[u, k].astype(F32), zero)

                def put(k, carry):
                    results[u, k] = tot.astype(BF16)
                    return carry

                lax.fori_loop(0, n, put, 0)
            else:
                def scan(k, a):
                    at = n - 1 - k if mode == "suffix" else k
                    results[u, at] = a.astype(BF16)
                    return a + stages[u, at].astype(F32)

                lax.fori_loop(0, n, scan, zero)
            peers(lambda p: phase2_desc(u, me, p).start())
            finals[u, pl.ds(pl.multiple_of(me * piece, piece), piece)] = results[u, me]

        owning(me, own)

    def by_owners(ref, sem, act):
        def of(count):
            return lambda: act(many(ref.at[pl.ds(0, count * piece)], sem))

        if owners == n:
            of(n - 1)()
        else:
            pl.when(me < owners)(of(owners - 1))
            pl.when(me >= owners)(of(owners))

    def phase2_wait(u):
        by_owners(finals.at[u], p2_r.at[u], lambda c: c.wait_recv())

    def exchange_sends_done(u, src):
        by_owners(src, p1_s.at[u], lambda c: c.wait_send())
        owning(me, lambda: many(results.at[u, pl.ds(0, n - 1)], p2_s.at[u]).wait_send())

    def chunk_desc(u, buf, b, j, per, send, recv, to):
        ref = buf.at[pl.ds(pl.multiple_of((b * per + j) * CHUNK, CHUNK), CHUNK)]
        return remote(ref, ref, send, recv, to)

    def loop(lo, hi, body):
        def one(k, carry):
            body(k)
            return carry

        lax.fori_loop(lo, hi, one, 0)

    def gather(u, buf, rows):
        per = rows // CHUNK

        def got(z, y, j):
            sem = ag_r.at[u, (z * 2 + y) * per + j]
            b = z * 4 + y * 2 + ci
            chunk_desc(u, buf, b, j, per, agy_s.at[u], sem, ypeer).wait_recv()

        def go(send, z, y, j, to):
            sem = ag_r.at[u, (z * 2 + y) * per + j]
            chunk_desc(u, buf, z * 4 + y * 2 + ci, j, per, send, sem, to).start()

        def to_core(z, y, j):
            b = z * 4 + y * 2 + ci
            chunk_desc(u, buf, b, j, per, agc_s.at[u], agc_r.at[u], cpeer).start()

        def up(z, j):
            pl.when(zi < planes - 1)(lambda: go(agz_s.at[u, z * per + j], z, yi, j, me + 4))

        def down(z, j):
            at = (planes + z) * per + j
            pl.when(zi > 0)(lambda: go(agz_s.at[u, at], z, yi, j, me - 4))

        def across(z, j):
            go(agy_s.at[u], z, yi, j, ypeer)
            to_core(z, yi, j)

        def own(j):
            up(zi, j)
            down(zi, j)
            across(zi, j)

        loop(0, per, own)

        def from_y(z, j):
            got(z, 1 - yi, j)
            to_core(z, 1 - yi, j)

        def away(d):
            def one(j):
                @pl.when(zi - d >= 0)
                def _():
                    got(zi - d, yi, j)
                    up(zi - d, j)
                    across(zi - d, j)

                @pl.when(zi + d < planes)
                def _():
                    got(zi + d, yi, j)
                    down(zi + d, j)
                    across(zi + d, j)

            loop(0, per, one)

        def far_y(d):
            def one(j):
                pl.when(zi - d >= 0)(lambda: from_y(zi - d, j))
                pl.when(zi + d < planes)(lambda: from_y(zi + d, j))

            loop(0, per, one)

        def each(d):
            away(d)
            pl.when(d == 1)(lambda: loop(0, per, lambda j: from_y(zi, j)))
            pl.when(d > 1)(lambda: far_y(d - 1))

        loop(1, planes, each)
        far_y(planes - 1)
        many(buf.at[pl.ds(0, n // 2 * rows)], agc_r.at[u]).wait_recv()

    def gather_sends_done(u, buf, rows):
        per = rows // CHUNK

        def z_done(at):
            chunk_desc(u, buf, 0, 0, per, agz_s.at[u, at], agc_r.at[u], ypeer).wait_send()

        def one(k):
            z = k // per
            pl.when((zi < planes - 1) & (z <= zi))(lambda: z_done(k))
            pl.when((zi > 0) & (z >= zi))(lambda: z_done(planes * per + k))

        loop(0, planes * per, one)
        many(buf.at[pl.ds(0, n // 4 * rows)], agy_s.at[u]).wait_send()
        many(buf.at[pl.ds(0, n // 2 * rows)], agc_s.at[u]).wait_send()

    def a2a_desc(owner, to):
        return remote(
            hid_t.at[pl.ds(pl.multiple_of(to * part, part), part)],
            feats.at[:, pl.ds(pl.multiple_of(owner * tok, tok), tok)],
            a2a_s, a2a_r, to,
        )

    barrier = pltpu.get_barrier_semaphore()
    peers(lambda p: pl.semaphore_signal(barrier, inc=1, device_id={"dp": p}, device_id_type=MESH))

    span = PER * tok

    def group_q(g):
        return qs[g * span:(g + 1) * span]

    for g in range(GROUPS):
        q = group_q(g)
        gram[g * HD:(g + 1) * HD] = mm(q, q, ((0,), (0,))).astype(BF16)

    pl.semaphore_wait(barrier, n - 1)
    phase1_start(0, gram)

    def turn(k, carry):
        at = pl.multiple_of(k * HD, HD)
        hid_t[pl.ds(at, HD)] = hid[:, pl.ds(at, HD)].T
        return carry

    lax.fori_loop(0, feat // HD, turn, 0)
    peers(lambda p: a2a_desc(me, p).start())
    feats[:, pl.ds(pl.multiple_of(me * tok, tok), tok)] = hid_t[
        pl.ds(pl.multiple_of(me * part, part), part)
    ]

    row = lax.rem(lax.broadcasted_iota(jnp.int32, (span, tok), 0), tok)
    causal = row >= lax.broadcasted_iota(jnp.int32, (span, tok), 1)

    def forward(down, ups):
        step = min(1024, feat)

        def one(k, acc):
            at = pl.multiple_of(k * step, step)
            return acc + mm(hid[:, pl.ds(at, step)], down[pl.ds(at, step)])

        acc = lax.fori_loop(0, feat // step, one, jnp.zeros((tok, WIDTH), F32))
        latent_b[...] = acc.astype(BF16)
        errs = []
        for g in range(GROUPS):
            cols = slice(g * HD, (g + 1) * HD)
            recon = mm(latent_b[:, cols], ups[g])
            errs.append((keys[:, cols].astype(F32) - recon).astype(BF16))
        return errs

    def local_scores(errs, g):
        s = mm(group_q(g), errs[g], ((1,), (1,)))
        return jnp.where(causal, s, 0.0)

    def errors_grad(g, errs, local):
        cross = mm(errs[g], finals[0, g * HD:(g + 1) * HD])
        return (pair_scale * (local + cross)).astype(BF16)

    def gradients(errs, locals_, ups, gl, upl):
        for g in range(GROUPS):
            cols = slice(g * HD, (g + 1) * HD)
            ge = errors_grad(g, errs, locals_[g])
            lg = (-mm(ge, ups[g], ((1,), (1,)))).astype(BF16)
            gl[pl.ds(pl.multiple_of(me * tok, tok), tok), cols] = lg
            upl[cols] = (-mm(latent_b[:, cols], ge, ((0,), (0,)))).astype(BF16)

    def new_rows(old, gl):
        step = 1024

        def one(k, acc):
            at = pl.multiple_of(k * step, step)
            return acc + mm(feats[:, pl.ds(at, step)], gl[pl.ds(at, step)])

        acc = lax.fori_loop(0, total // step, one, jnp.zeros((part, WIDTH), F32))
        return (old.astype(F32) - RATE_DOWN * root * acc).astype(BF16)

    def new_up(old, u, g):
        grad = finals[u, g * HD:(g + 1) * HD].astype(F32)
        return (old.astype(F32) - RATE_UP * root * grad).astype(BF16)

    mine = pl.ds(pl.multiple_of(me * part, part), part)

    ups = [up0[g] for g in range(GROUPS)]
    errs = forward(down0, ups)
    phase2_start(0, gram, "suffix")
    locals_ = []
    for g in range(GROUPS):
        s = local_scores(errs, g).astype(BF16)
        locals_.append(mm(s, group_q(g), ((0,), (0,))))
    phase2_wait(0)
    gradients(errs, locals_, ups, gl1, upl1)
    phase1_start(1, upl1)
    gather(0, gl1, tok)
    many(feats.at[:, pl.ds(0, total - tok)], a2a_r).wait_recv()
    phase2_start(1, upl1, "sum")
    down1[mine] = new_rows(down0[mine], gl1)
    gather(1, down1, part)
    phase2_wait(1)

    ups = [new_up(up0[g], 1, g) for g in range(GROUPS)]
    errs = forward(down1, ups)
    for g in range(GROUPS):
        kgram[g * HD:(g + 1) * HD] = mm(errs[g], errs[g], ((0,), (0,))).astype(BF16)
    phase1_start(2, kgram)
    locals_ = []
    sums = jnp.zeros((tok, 1), F32)
    for g in range(GROUPS):
        s = local_scores(errs, g)
        own = jnp.sum(s * s, axis=1, keepdims=True)
        for h in range(PER):
            sums = sums + own[h * tok:(h + 1) * tok]
        locals_.append(mm(s.astype(BF16), group_q(g), ((0,), (0,))))
    gradients(errs, locals_, ups, gl2, upl2)
    phase1_start(3, upl2)
    phase2_start(2, kgram, "prefix")
    gather(2, gl2, tok)
    phase2_start(3, upl2, "sum")
    rows_out[...] = new_rows(down1[mine], gl2)
    phase2_wait(2)
    for g in range(GROUPS):
        q = group_q(g)
        moved = mm(q, finals[2, g * HD:(g + 1) * HD])
        far = jnp.sum(moved * q.astype(F32), axis=1, keepdims=True)
        for h in range(PER):
            sums = sums + far[h * tok:(h + 1) * tok]
    where = (me * tok + 1 + lax.broadcasted_iota(jnp.int32, (tok, 1), 0)).astype(F32)
    err_out[...] = sums / (where * HEADS)
    phase2_wait(3)
    for g in range(GROUPS):
        up_out[g] = new_up(ups[g], 3, g)

    many(hid_t.at[pl.ds(0, feat - part)], a2a_s).wait_send()
    exchange_sends_done(0, gram)
    exchange_sends_done(1, upl1)
    exchange_sends_done(2, kgram)
    exchange_sends_done(3, upl2)
    gather_sends_done(0, gl1, tok)
    gather_sends_done(1, down1, part)
    gather_sends_done(2, gl2, tok)


def shards(hidden_rows, queries, keys, down_basis, up_basis, head_group):
    tok, feat = hidden_rows.shape
    n = lax.axis_size("dp")
    part = feat // n
    piece = WIDTH // min(n, WIDTH // 16)
    chunks = max(feat, n * tok) // CHUNK
    heads = jnp.arange(HEADS, dtype=jnp.int32)
    same = head_group[:, None] == head_group[None, :]
    before = jnp.sum((same & (heads[None, :] < heads[:, None])).astype(jnp.int32), axis=1)
    place = head_group * PER + before
    order = jnp.sum(jnp.where(place[None, :] == heads[:, None], heads[None, :], 0), axis=1)
    vmem = pl.BlockSpec(memory_space=pltpu.VMEM)
    dma = pltpu.SemaphoreType.DMA
    qs = pl.pallas_call(
        sort_heads,
        out_shape=jax.ShapeDtypeStruct((HEADS * tok, HD), BF16),
        in_specs=[pl.BlockSpec(memory_space=pltpu.SMEM), vmem],
        out_specs=vmem,
    )(order, queries)
    rows, up, err = pl.pallas_call(
        functools.partial(kernel, n, tok, feat),
        out_shape=(
            jax.ShapeDtypeStruct((part, WIDTH), BF16),
            jax.ShapeDtypeStruct((GROUPS, HD, HD), BF16),
            jax.ShapeDtypeStruct((tok, 1), F32),
        ),
        in_specs=[vmem] * 5,
        out_specs=(vmem, vmem, vmem),
        scratch_shapes=[
            pltpu.VMEM((feat, tok), BF16),
            pltpu.VMEM((part, n * tok), BF16),
            pltpu.VMEM((tok, WIDTH), BF16),
            pltpu.VMEM((n * tok, WIDTH), BF16),
            pltpu.VMEM((n * tok, WIDTH), BF16),
            pltpu.VMEM((feat, WIDTH), BF16),
            pltpu.VMEM((WIDTH, HD), BF16),
            pltpu.VMEM((WIDTH, HD), BF16),
            pltpu.VMEM((WIDTH, HD), BF16),
            pltpu.VMEM((WIDTH, HD), BF16),
            pltpu.VMEM((4, n, piece, HD), BF16),
            pltpu.VMEM((4, n, piece, HD), BF16),
            pltpu.VMEM((4, WIDTH, HD), BF16),
            dma, dma,
            dma((4,)), dma((4,)), dma((4,)), dma((4,)),
            dma((3, chunks // 2)), dma((3,)), dma((3,)), dma((3,)), dma((3, chunks // 2)),
        ],
        compiler_params=pltpu.CompilerParams(
            collective_id=0, has_side_effects=True, vmem_limit_bytes=48 * 1024 * 1024
        ),
    )(hidden_rows, qs, keys, down_basis, up_basis)
    return rows, up, err.reshape(tok)


def solution(mesh):
    return jax.shard_map(
        shards,
        mesh=mesh,
        in_specs=(
            P(("parts", "dp"), None),
            P(("parts", "dp"), None),
            P(("parts", "dp"), None),
            P("parts", None),
            P("parts", None, None),
            P(),
        ),
        out_specs=(P(("parts", "dp"), None), P("parts", None, None), P(("parts", "dp"))),
        check_vma=False,
    )
```

```python
import functools
import math

import jax
import jax.numpy as jnp
from jax import lax
from jax.experimental import pallas as pl
from jax.experimental.pallas import tpu as pltpu
from jax.sharding import PartitionSpec as P

HEADS = 32
GROUPS = 4
HD = 128
PER = HEADS // GROUPS
WIDTH = GROUPS * HD
CHUNK = 64
RATE_DOWN = 1.0
RATE_UP = 8.0
F32 = jnp.float32
BF16 = jnp.bfloat16
MESH = pl.DeviceIdType.MESH


def mm(a, b, dims=((1,), (0,))):
    return lax.dot_general(a, b, (dims, ((), ())), preferred_element_type=F32)


def sort_heads(order, queries, qs):
    tok = queries.shape[0]
    for s in range(HEADS):
        col = pl.multiple_of(order[s] * HD, HD)
        qs[s * tok:(s + 1) * tok] = queries[:, pl.ds(col, HD)]


def kernel(
    n, tok, feat,
    hid, qs, keys, down0, up0,
    rows_out, up_out, err_out,
    hid_t, feats, latent_b, gl1, gl2, down1, gram, kgram, upl1, upl2,
    stages_gram, stages_up, results, finals,
    a2a_s, a2a_r, p1_s, p1_r, p2_s, p2_r, agz_s, agy_s, agc_s, agc_r, ag_r,
):
    me = lax.axis_index("dp")
    planes = n // 4
    zi, yi, ci = me // 4, lax.rem(me // 2, 2), lax.rem(me, 2)
    ypeer = zi * 4 + (1 - yi) * 2 + ci
    cpeer = zi * 4 + yi * 2 + (1 - ci)
    part = feat // n
    owners = min(n, WIDTH // 16)
    piece = WIDTH // owners
    total = n * tok
    pair_scale = 2.0 / (total * total * HEADS)
    root = math.sqrt(total)

    def remote(src, dst, s, r, to):
        return pltpu.make_async_remote_copy(
            src_ref=src, dst_ref=dst, send_sem=s, recv_sem=r,
            device_id={"dp": to}, device_id_type=MESH,
        )

    def many(ref, sem):
        return remote(ref, ref, sem, sem, cpeer)

    def peers(body):
        def one(k, carry):
            body(lax.rem(me + k, n))
            return carry

        lax.fori_loop(1, n, one, 0)

    def owning(p, body):
        if owners == n:
            body()
        else:
            pl.when(p < owners)(body)

    def stage(u):
        return (stages_up if u % 2 else stages_gram).at[u // 2]

    def phase1_desc(u, src, owner, to):
        return remote(
            src.at[pl.ds(pl.multiple_of(to * piece, piece), piece)],
            stage(u).at[owner], p1_s.at[u], p1_r.at[u], to,
        )

    def phase1_start(u, src):
        peers(lambda p: owning(p, lambda: phase1_desc(u, src, me, p).start()))

        def keep():
            stage(u)[me] = src[pl.ds(pl.multiple_of(me * piece, piece), piece)]

        owning(me, keep)

    def phase2_desc(u, owner, to):
        return remote(
            results.at[u, to],
            finals.at[u, pl.ds(pl.multiple_of(owner * piece, piece), piece)],
            p2_s.at[u], p2_r.at[u], to,
        )

    def phase2_start(u, src, mode):
        def own():
            many(stage(u).at[pl.ds(0, n - 1)], p1_r.at[u]).wait_recv()
            zero = jnp.zeros((piece, HD), F32)
            if u % 2:
                tot = lax.fori_loop(0, n, lambda k, a: a + stage(u)[k].astype(F32), zero)

                old = mode[pl.ds(pl.multiple_of(me * piece, piece), piece)].astype(F32)
                new = (old - RATE_UP * root * tot).astype(BF16)

                def put(k, carry):
                    results[u, k] = new
                    return carry

                lax.fori_loop(0, n, put, 0)
            else:
                def scan(k, a):
                    at = n - 1 - k if mode == "suffix" else k
                    results[u, at] = a.astype(BF16)
                    return a + stage(u)[at].astype(F32)

                lax.fori_loop(0, n, scan, zero)
            peers(lambda p: phase2_desc(u, me, p).start())
            finals[u, pl.ds(pl.multiple_of(me * piece, piece), piece)] = results[u, me]

        owning(me, own)

    def by_owners(ref, sem, act):
        def of(count):
            return lambda: act(many(ref.at[pl.ds(0, count * piece)], sem))

        if owners == n:
            of(n - 1)()
        else:
            pl.when(me < owners)(of(owners - 1))
            pl.when(me >= owners)(of(owners))

    def phase2_wait(u):
        by_owners(finals.at[u], p2_r.at[u], lambda c: c.wait_recv())

    def exchange_sends_done(u, src):
        by_owners(src, p1_s.at[u], lambda c: c.wait_send())
        owning(me, lambda: many(results.at[u, pl.ds(0, n - 1)], p2_s.at[u]).wait_send())

    def chunk_desc(u, buf, b, j, per, send, recv, to):
        ref = buf.at[pl.ds(pl.multiple_of((b * per + j) * CHUNK, CHUNK), CHUNK)]
        return remote(ref, ref, send, recv, to)

    def loop(lo, hi, body):
        def one(k, carry):
            body(k)
            return carry

        lax.fori_loop(lo, hi, one, 0)

    def gather(u, buf, rows):
        per = rows // CHUNK

        def got(z, y, j):
            sem = ag_r.at[u, (z * 2 + y) * per + j]
            b = z * 4 + y * 2 + ci
            chunk_desc(u, buf, b, j, per, agy_s.at[u], sem, ypeer).wait_recv()

        def go(send, z, y, j, to):
            sem = ag_r.at[u, (z * 2 + y) * per + j]
            chunk_desc(u, buf, z * 4 + y * 2 + ci, j, per, send, sem, to).start()

        def to_core(z, y, j):
            b = z * 4 + y * 2 + ci
            chunk_desc(u, buf, b, j, per, agc_s.at[u], agc_r.at[u], cpeer).start()

        def up(z, j):
            pl.when(zi < planes - 1)(lambda: go(agz_s.at[u, z * per + j], z, yi, j, me + 4))

        def down(z, j):
            at = (planes + z) * per + j
            pl.when(zi > 0)(lambda: go(agz_s.at[u, at], z, yi, j, me - 4))

        def across(z, j):
            go(agy_s.at[u], z, yi, j, ypeer)
            to_core(z, yi, j)

        def own(j):
            up(zi, j)
            down(zi, j)
            across(zi, j)

        loop(0, per, own)

        def from_y(z, j):
            got(z, 1 - yi, j)
            to_core(z, 1 - yi, j)

        def away(d):
            def one(j):
                @pl.when(zi - d >= 0)
                def _():
                    got(zi - d, yi, j)
                    up(zi - d, j)
                    across(zi - d, j)

                @pl.when(zi + d < planes)
                def _():
                    got(zi + d, yi, j)
                    down(zi + d, j)
                    across(zi + d, j)

            loop(0, per, one)

        def far_y(d):
            def one(j):
                pl.when(zi - d >= 0)(lambda: from_y(zi - d, j))
                pl.when(zi + d < planes)(lambda: from_y(zi + d, j))

            loop(0, per, one)

        def each(d):
            away(d)
            pl.when(d == 1)(lambda: loop(0, per, lambda j: from_y(zi, j)))
            pl.when(d > 1)(lambda: far_y(d - 1))

        loop(1, planes, each)
        far_y(planes - 1)
        many(buf.at[pl.ds(0, n // 2 * rows)], agc_r.at[u]).wait_recv()

    def gather_sends_done(u, buf, rows):
        per = rows // CHUNK

        def z_done(at):
            chunk_desc(u, buf, 0, 0, per, agz_s.at[u, at], agc_r.at[u], ypeer).wait_send()

        def one(k):
            z = k // per
            pl.when((zi < planes - 1) & (z <= zi))(lambda: z_done(k))
            pl.when((zi > 0) & (z >= zi))(lambda: z_done(planes * per + k))

        loop(0, planes * per, one)
        many(buf.at[pl.ds(0, n // 4 * rows)], agy_s.at[u]).wait_send()
        many(buf.at[pl.ds(0, n // 2 * rows)], agc_s.at[u]).wait_send()

    def a2a_desc(owner, to):
        return remote(
            hid_t.at[pl.ds(pl.multiple_of(to * part, part), part)],
            feats.at[:, pl.ds(pl.multiple_of(owner * tok, tok), tok)],
            a2a_s, a2a_r, to,
        )

    barrier = pltpu.get_barrier_semaphore()
    peers(lambda p: pl.semaphore_signal(barrier, inc=1, device_id={"dp": p}, device_id_type=MESH))

    span = PER * tok

    def group_q(g):
        return qs[g * span:(g + 1) * span]

    for g in range(GROUPS):
        q = group_q(g)
        gram[g * HD:(g + 1) * HD] = mm(q, q, ((0,), (0,))).astype(BF16)

    pl.semaphore_wait(barrier, n - 1)
    phase1_start(0, gram)

    def turn(k, carry):
        at = pl.multiple_of(k * HD, HD)
        hid_t[pl.ds(at, HD)] = hid[:, pl.ds(at, HD)].T
        return carry

    lax.fori_loop(0, feat // HD, turn, 0)
    feats[:, pl.ds(pl.multiple_of(me * tok, tok), tok)] = hid_t[
        pl.ds(pl.multiple_of(me * part, part), part)
    ]

    row = lax.rem(lax.broadcasted_iota(jnp.int32, (span, tok), 0), tok)
    causal = row >= lax.broadcasted_iota(jnp.int32, (span, tok), 1)

    def forward(down, ups):
        step = min(1024, feat)

        def one(k, acc):
            at = pl.multiple_of(k * step, step)
            return acc + mm(hid[:, pl.ds(at, step)], down[pl.ds(at, step)])

        acc = lax.fori_loop(0, feat // step, one, jnp.zeros((tok, WIDTH), F32))
        latent_b[...] = acc.astype(BF16)
        errs = []
        for g in range(GROUPS):
            cols = slice(g * HD, (g + 1) * HD)
            recon = mm(latent_b[:, cols], ups[g])
            errs.append((keys[:, cols].astype(F32) - recon).astype(BF16))
        return errs

    def local_scores(errs, g):
        s = mm(group_q(g), errs[g], ((1,), (1,)))
        return jnp.where(causal, s, 0.0)

    def errors_grad(g, errs, local):
        cross = mm(errs[g], finals[0, g * HD:(g + 1) * HD])
        return (pair_scale * (local + cross)).astype(BF16)

    def gradients(errs, locals_, ups, gl, upl):
        for g in range(GROUPS):
            cols = slice(g * HD, (g + 1) * HD)
            ge = errors_grad(g, errs, locals_[g])
            lg = (-mm(ge, ups[g], ((1,), (1,)))).astype(BF16)
            gl[pl.ds(pl.multiple_of(me * tok, tok), tok), cols] = lg
            upl[cols] = (-mm(latent_b[:, cols], ge, ((0,), (0,)))).astype(BF16)

    def new_rows(old, gl):
        step = 1024

        def one(k, acc):
            at = pl.multiple_of(k * step, step)
            return acc + mm(feats[:, pl.ds(at, step)], gl[pl.ds(at, step)])

        acc = lax.fori_loop(0, total // step, one, jnp.zeros((part, WIDTH), F32))
        return (old.astype(F32) - RATE_DOWN * root * acc).astype(BF16)

    mine = pl.ds(pl.multiple_of(me * part, part), part)

    ups = [up0[g * HD:(g + 1) * HD] for g in range(GROUPS)]
    errs = forward(down0, ups)
    phase2_start(0, gram, "suffix")
    peers(lambda p: a2a_desc(me, p).start())
    locals_ = []
    for g in range(GROUPS):
        s = local_scores(errs, g).astype(BF16)
        locals_.append(mm(s, group_q(g), ((0,), (0,))))
    phase2_wait(0)
    gradients(errs, locals_, ups, gl1, upl1)
    phase1_start(1, upl1)
    gather(0, gl1, tok)
    many(feats.at[:, pl.ds(0, total - tok)], a2a_r).wait_recv()
    phase2_start(1, upl1, up0)
    down1[mine] = new_rows(down0[mine], gl1)
    gather(1, down1, part)
    phase2_wait(1)

    ups = [finals[1, g * HD:(g + 1) * HD] for g in range(GROUPS)]
    errs = forward(down1, ups)
    for g in range(GROUPS):
        kgram[g * HD:(g + 1) * HD] = mm(errs[g], errs[g], ((0,), (0,))).astype(BF16)
    phase1_start(2, kgram)
    locals_ = []
    sums = jnp.zeros((tok, 1), F32)
    for g in range(GROUPS):
        s = local_scores(errs, g)
        own = jnp.sum(s * s, axis=1, keepdims=True)
        for h in range(PER):
            sums = sums + own[h * tok:(h + 1) * tok]
        locals_.append(mm(s.astype(BF16), group_q(g), ((0,), (0,))))
    gradients(errs, locals_, ups, gl2, upl2)
    phase1_start(3, upl2)
    phase2_start(2, kgram, "prefix")
    gather(2, gl2, tok)
    phase2_start(3, upl2, finals.at[1])
    rows_out[...] = new_rows(down1[mine], gl2)
    phase2_wait(2)
    for g in range(GROUPS):
        q = group_q(g)
        moved = mm(q, finals[2, g * HD:(g + 1) * HD])
        far = jnp.sum(moved * q.astype(F32), axis=1, keepdims=True)
        for h in range(PER):
            sums = sums + far[h * tok:(h + 1) * tok]
    where = (me * tok + 1 + lax.broadcasted_iota(jnp.int32, (tok, 1), 0)).astype(F32)
    err_out[...] = sums / (where * HEADS)
    phase2_wait(3)
    up_out[...] = finals[3]

    many(hid_t.at[pl.ds(0, feat - part)], a2a_s).wait_send()
    exchange_sends_done(0, gram)
    exchange_sends_done(1, upl1)
    exchange_sends_done(2, kgram)
    exchange_sends_done(3, upl2)
    gather_sends_done(0, gl1, tok)
    gather_sends_done(1, down1, part)
    gather_sends_done(2, gl2, tok)


def shards(hidden_rows, queries, keys, down_basis, up_basis, head_group):
    tok, feat = hidden_rows.shape
    n = lax.axis_size("dp")
    part = feat // n
    piece = WIDTH // min(n, WIDTH // 16)
    chunks = max(feat, n * tok) // CHUNK
    heads = jnp.arange(HEADS, dtype=jnp.int32)
    same = head_group[:, None] == head_group[None, :]
    before = jnp.sum((same & (heads[None, :] < heads[:, None])).astype(jnp.int32), axis=1)
    place = head_group * PER + before
    order = jnp.sum(jnp.where(place[None, :] == heads[:, None], heads[None, :], 0), axis=1)
    vmem = pl.BlockSpec(memory_space=pltpu.VMEM)
    dma = pltpu.SemaphoreType.DMA
    qs = pl.pallas_call(
        sort_heads,
        out_shape=jax.ShapeDtypeStruct((HEADS * tok, HD), BF16),
        in_specs=[pl.BlockSpec(memory_space=pltpu.SMEM), vmem],
        out_specs=vmem,
    )(order, queries)
    rows, up, err = pl.pallas_call(
        functools.partial(kernel, n, tok, feat),
        out_shape=(
            jax.ShapeDtypeStruct((part, WIDTH), BF16),
            jax.ShapeDtypeStruct((WIDTH, HD), BF16),
            jax.ShapeDtypeStruct((tok, 1), F32),
        ),
        in_specs=[vmem] * 5,
        out_specs=(vmem, vmem, vmem),
        scratch_shapes=[
            pltpu.VMEM((feat, tok), BF16),
            pltpu.VMEM((part, n * tok), BF16),
            pltpu.VMEM((tok, WIDTH), BF16),
            pltpu.VMEM((n * tok, WIDTH), BF16),
            pltpu.VMEM((n * tok, WIDTH), BF16),
            pltpu.VMEM((feat, WIDTH), BF16),
            pltpu.VMEM((WIDTH, HD), BF16),
            pltpu.VMEM((WIDTH, HD), BF16),
            pltpu.VMEM((WIDTH, HD), BF16),
            pltpu.VMEM((WIDTH, HD), BF16),
            pltpu.VMEM((2, n, piece, HD), BF16),
            pltpu.VMEM((2, n, piece, HD), BF16),
            pltpu.VMEM((4, n, piece, HD), BF16),
            pltpu.VMEM((4, WIDTH, HD), BF16),
            dma, dma,
            dma((4,)), dma((4,)), dma((4,)), dma((4,)),
            dma((3, chunks // 2)), dma((3,)), dma((3,)), dma((3,)), dma((3, chunks // 2)),
        ],
        compiler_params=pltpu.CompilerParams(
            collective_id=0, has_side_effects=True, vmem_limit_bytes=48 * 1024 * 1024
        ),
    )(hidden_rows, qs, keys, down_basis, up_basis.reshape(WIDTH, HD))
    return rows, up.reshape(GROUPS, HD, HD), err.reshape(tok)


def solution(mesh):
    return jax.shard_map(
        shards,
        mesh=mesh,
        in_specs=(
            P(("parts", "dp"), None),
            P(("parts", "dp"), None),
            P(("parts", "dp"), None),
            P("parts", None),
            P("parts", None, None),
            P(),
        ),
        out_specs=(P(("parts", "dp"), None), P("parts", None, None), P(("parts", "dp"))),
        check_vma=False,
    )
```

```python
import functools
import math

import jax
import jax.numpy as jnp
from jax import lax
from jax.experimental import pallas as pl
from jax.experimental.pallas import tpu as pltpu
from jax.sharding import PartitionSpec as P

HEADS = 32
GROUPS = 4
HD = 128
PER = HEADS // GROUPS
WIDTH = GROUPS * HD
CHUNK = 64
RATE_DOWN = 1.0
RATE_UP = 8.0
F32 = jnp.float32
BF16 = jnp.bfloat16
MESH = pl.DeviceIdType.MESH


def mm(a, b, dims=((1,), (0,))):
    return lax.dot_general(a, b, (dims, ((), ())), preferred_element_type=F32)


def sort_heads(order, queries, qs):
    tok = queries.shape[0]
    for s in range(HEADS):
        col = pl.multiple_of(order[s] * HD, HD)
        qs[s * tok:(s + 1) * tok] = queries[:, pl.ds(col, HD)]


def kernel(
    n, tok, feat,
    hid, qs, keys, down0, up0,
    rows_out, up_out, err_out,
    hid_t, feats, latent_b, gl1, gl2, down1, gram, kgram, upl1, upl2,
    stages_gram, stages_up, results, finals,
    a2a_s, a2a_r, p1_s, p1_r, p2_s, p2_r, agz_s, agy_s, agc_s, agc_r, ag_r,
):
    me = lax.axis_index("dp")
    planes = n // 4
    zi, yi, ci = me // 4, lax.rem(me // 2, 2), lax.rem(me, 2)
    ypeer = zi * 4 + (1 - yi) * 2 + ci
    cpeer = zi * 4 + yi * 2 + (1 - ci)
    part = feat // n
    owners = min(n, WIDTH // 16)
    piece = WIDTH // owners
    total = n * tok
    pair_scale = 2.0 / (total * total * HEADS)
    root = math.sqrt(total)

    def remote(src, dst, s, r, to):
        return pltpu.make_async_remote_copy(
            src_ref=src, dst_ref=dst, send_sem=s, recv_sem=r,
            device_id={"dp": to}, device_id_type=MESH,
        )

    def many(ref, sem):
        return remote(ref, ref, sem, sem, cpeer)

    def peers(body):
        def one(k, carry):
            body(lax.rem(me + k, n))
            return carry

        lax.fori_loop(1, n, one, 0)

    def owning(p, body):
        if owners == n:
            body()
        else:
            pl.when(p < owners)(body)

    def stage(u):
        return (stages_up if u % 2 else stages_gram).at[u // 2]

    def phase1_desc(u, src, owner, to):
        return remote(
            src.at[pl.ds(pl.multiple_of(to * piece, piece), piece)],
            stage(u).at[owner], p1_s.at[u], p1_r.at[u], to,
        )

    def phase1_start(u, src):
        peers(lambda p: owning(p, lambda: phase1_desc(u, src, me, p).start()))

        def keep():
            stage(u)[me] = src[pl.ds(pl.multiple_of(me * piece, piece), piece)]

        owning(me, keep)

    def phase2_desc(u, owner, to):
        return remote(
            results.at[u, to],
            finals.at[u, pl.ds(pl.multiple_of(owner * piece, piece), piece)],
            p2_s.at[u], p2_r.at[u], to,
        )

    def phase2_start(u, src, mode):
        def own():
            many(stage(u).at[pl.ds(0, n - 1)], p1_r.at[u]).wait_recv()
            zero = jnp.zeros((piece, HD), F32)
            if u % 2:
                tot = lax.fori_loop(0, n, lambda k, a: a + stage(u)[k].astype(F32), zero)

                old = mode[pl.ds(pl.multiple_of(me * piece, piece), piece)].astype(F32)
                new = (old - RATE_UP * root * tot).astype(BF16)

                def put(k, carry):
                    results[u, k] = new
                    return carry

                lax.fori_loop(0, n, put, 0)
            else:
                def scan(k, a):
                    at = n - 1 - k if mode == "suffix" else k
                    results[u, at] = a.astype(BF16)
                    return a + stage(u)[at].astype(F32)

                lax.fori_loop(0, n, scan, zero)
            peers(lambda p: phase2_desc(u, me, p).start())
            finals[u, pl.ds(pl.multiple_of(me * piece, piece), piece)] = results[u, me]

        owning(me, own)

    def by_owners(ref, sem, act):
        def of(count):
            return lambda: act(many(ref.at[pl.ds(0, count * piece)], sem))

        if owners == n:
            of(n - 1)()
        else:
            pl.when(me < owners)(of(owners - 1))
            pl.when(me >= owners)(of(owners))

    def phase2_wait(u):
        by_owners(finals.at[u], p2_r.at[u], lambda c: c.wait_recv())

    def exchange_sends_done(u, src):
        by_owners(src, p1_s.at[u], lambda c: c.wait_send())
        owning(me, lambda: many(results.at[u, pl.ds(0, n - 1)], p2_s.at[u]).wait_send())

    def chunk_desc(u, buf, b, j, per, send, recv, to):
        ref = buf.at[pl.ds(pl.multiple_of((b * per + j) * CHUNK, CHUNK), CHUNK)]
        return remote(ref, ref, send, recv, to)

    def loop(lo, hi, body):
        def one(k, carry):
            body(k)
            return carry

        lax.fori_loop(lo, hi, one, 0)

    def gather(u, buf, rows):
        per = rows // CHUNK

        def got(z, y, j):
            sem = ag_r.at[u, (z * 2 + y) * per + j]
            b = z * 4 + y * 2 + ci
            chunk_desc(u, buf, b, j, per, agy_s.at[u], sem, ypeer).wait_recv()

        def go(send, z, y, j, to):
            sem = ag_r.at[u, (z * 2 + y) * per + j]
            chunk_desc(u, buf, z * 4 + y * 2 + ci, j, per, send, sem, to).start()

        def to_core(z, y, j):
            b = z * 4 + y * 2 + ci
            chunk_desc(u, buf, b, j, per, agc_s.at[u], agc_r.at[u], cpeer).start()

        def up(z, j):
            pl.when(zi < planes - 1)(lambda: go(agz_s.at[u, z * per + j], z, yi, j, me + 4))

        def down(z, j):
            at = (planes + z) * per + j
            pl.when(zi > 0)(lambda: go(agz_s.at[u, at], z, yi, j, me - 4))

        def across(z, j):
            go(agy_s.at[u], z, yi, j, ypeer)
            to_core(z, yi, j)

        def own(j):
            up(zi, j)
            down(zi, j)
            across(zi, j)

        loop(0, per, own)

        def from_y(z, j):
            got(z, 1 - yi, j)
            to_core(z, 1 - yi, j)

        def away(d):
            def one(j):
                @pl.when(zi - d >= 0)
                def _():
                    got(zi - d, yi, j)
                    up(zi - d, j)
                    across(zi - d, j)

                @pl.when(zi + d < planes)
                def _():
                    got(zi + d, yi, j)
                    down(zi + d, j)
                    across(zi + d, j)

            loop(0, per, one)

        def far_y(d):
            def one(j):
                pl.when(zi - d >= 0)(lambda: from_y(zi - d, j))
                pl.when(zi + d < planes)(lambda: from_y(zi + d, j))

            loop(0, per, one)

        def each(d):
            away(d)
            pl.when(d == 1)(lambda: loop(0, per, lambda j: from_y(zi, j)))
            pl.when(d > 1)(lambda: far_y(d - 1))

        loop(1, planes, each)
        far_y(planes - 1)
        many(buf.at[pl.ds(0, n // 2 * rows)], agc_r.at[u]).wait_recv()

    def gather_sends_done(u, buf, rows):
        per = rows // CHUNK

        def z_done(at):
            chunk_desc(u, buf, 0, 0, per, agz_s.at[u, at], agc_r.at[u], ypeer).wait_send()

        def one(k):
            z = k // per
            pl.when((zi < planes - 1) & (z <= zi))(lambda: z_done(k))
            pl.when((zi > 0) & (z >= zi))(lambda: z_done(planes * per + k))

        loop(0, planes * per, one)
        many(buf.at[pl.ds(0, n // 4 * rows)], agy_s.at[u]).wait_send()
        many(buf.at[pl.ds(0, n // 2 * rows)], agc_s.at[u]).wait_send()

    def a2a_desc(owner, to):
        return remote(
            hid_t.at[pl.ds(pl.multiple_of(to * part, part), part)],
            feats.at[:, pl.ds(pl.multiple_of(owner * tok, tok), tok)],
            a2a_s, a2a_r, to,
        )

    barrier = pltpu.get_barrier_semaphore()
    peers(lambda p: pl.semaphore_signal(barrier, inc=1, device_id={"dp": p}, device_id_type=MESH))

    span = PER * tok

    def group_q(g):
        return qs[g * span:(g + 1) * span]

    for g in range(GROUPS):
        q = group_q(g)
        gram[g * HD:(g + 1) * HD] = mm(q, q, ((0,), (0,))).astype(BF16)

    pl.semaphore_wait(barrier, n - 1)
    phase1_start(0, gram)

    def turn(k, carry):
        at = pl.multiple_of(k * HD, HD)
        hid_t[pl.ds(at, HD)] = hid[:, pl.ds(at, HD)].T
        return carry

    lax.fori_loop(0, feat // HD, turn, 0)
    feats[:, pl.ds(pl.multiple_of(me * tok, tok), tok)] = hid_t[
        pl.ds(pl.multiple_of(me * part, part), part)
    ]

    row = lax.rem(lax.broadcasted_iota(jnp.int32, (span, tok), 0), tok)
    causal = row >= lax.broadcasted_iota(jnp.int32, (span, tok), 1)

    def forward(down, ups):
        step = min(1024, feat)

        def one(k, acc):
            at = pl.multiple_of(k * step, step)
            return acc + mm(hid[:, pl.ds(at, step)], down[pl.ds(at, step)])

        acc = lax.fori_loop(0, feat // step, one, jnp.zeros((tok, WIDTH), F32))
        latent_b[...] = acc.astype(BF16)
        errs = []
        for g in range(GROUPS):
            cols = slice(g * HD, (g + 1) * HD)
            recon = mm(latent_b[:, cols], ups[g])
            errs.append((keys[:, cols].astype(F32) - recon).astype(BF16))
        return errs

    def local_scores(errs, g):
        s = mm(group_q(g), errs[g], ((1,), (1,)))
        return jnp.where(causal, s, 0.0)

    def errors_grad(g, errs, local):
        cross = mm(errs[g], finals[0, g * HD:(g + 1) * HD])
        return (pair_scale * (local + cross)).astype(BF16)

    def gradients(errs, locals_, ups, gl, upl):
        for g in range(GROUPS):
            cols = slice(g * HD, (g + 1) * HD)
            ge = errors_grad(g, errs, locals_[g])
            lg = (-mm(ge, ups[g], ((1,), (1,)))).astype(BF16)
            gl[pl.ds(pl.multiple_of(me * tok, tok), tok), cols] = lg
            upl[cols] = (-mm(latent_b[:, cols], ge, ((0,), (0,)))).astype(BF16)

    def new_rows(old, gl):
        step = 1024

        def one(k, acc):
            at = pl.multiple_of(k * step, step)
            return acc + mm(feats[:, pl.ds(at, step)], gl[pl.ds(at, step)])

        acc = lax.fori_loop(0, total // step, one, jnp.zeros((part, WIDTH), F32))
        return (old.astype(F32) - RATE_DOWN * root * acc).astype(BF16)

    mine = pl.ds(pl.multiple_of(me * part, part), part)

    ups = [up0[g * HD:(g + 1) * HD] for g in range(GROUPS)]
    errs = forward(down0, ups)
    phase2_start(0, gram, "suffix")
    peers(lambda p: a2a_desc(me, p).start())
    locals_ = []
    for g in range(GROUPS):
        s = local_scores(errs, g).astype(BF16)
        locals_.append(mm(s, group_q(g), ((0,), (0,))))
    phase2_wait(0)
    gradients(errs, locals_, ups, gl1, upl1)
    phase1_start(1, upl1)
    gather(0, gl1, tok)
    many(feats.at[:, pl.ds(0, total - tok)], a2a_r).wait_recv()
    phase2_start(1, upl1, up0)
    down1[mine] = new_rows(down0[mine], gl1)
    gather(1, down1, part)
    phase2_wait(1)

    ups = [finals[1, g * HD:(g + 1) * HD] for g in range(GROUPS)]
    errs = forward(down1, ups)
    for g in range(GROUPS):
        kgram[g * HD:(g + 1) * HD] = mm(errs[g], errs[g], ((0,), (0,))).astype(BF16)
    phase1_start(2, kgram)
    locals_ = []
    sums = jnp.zeros((tok, 1), F32)
    for g in range(GROUPS):
        s = local_scores(errs, g)
        own = jnp.sum(s * s, axis=1, keepdims=True)
        for h in range(PER):
            sums = sums + own[h * tok:(h + 1) * tok]
        locals_.append(mm(s.astype(BF16), group_q(g), ((0,), (0,))))
    phase2_start(2, kgram, "prefix")
    gradients(errs, locals_, ups, gl2, upl2)
    phase1_start(3, upl2)
    gather(2, gl2, tok)
    phase2_start(3, upl2, finals.at[1])
    rows_out[...] = new_rows(down1[mine], gl2)
    phase2_wait(2)
    for g in range(GROUPS):
        q = group_q(g)
        moved = mm(q, finals[2, g * HD:(g + 1) * HD])
        far = jnp.sum(moved * q.astype(F32), axis=1, keepdims=True)
        for h in range(PER):
            sums = sums + far[h * tok:(h + 1) * tok]
    where = (me * tok + 1 + lax.broadcasted_iota(jnp.int32, (tok, 1), 0)).astype(F32)
    err_out[...] = sums / (where * HEADS)
    phase2_wait(3)
    up_out[...] = finals[3]

    many(hid_t.at[pl.ds(0, feat - part)], a2a_s).wait_send()
    exchange_sends_done(0, gram)
    exchange_sends_done(1, upl1)
    exchange_sends_done(2, kgram)
    exchange_sends_done(3, upl2)
    gather_sends_done(0, gl1, tok)
    gather_sends_done(1, down1, part)
    gather_sends_done(2, gl2, tok)


def shards(hidden_rows, queries, keys, down_basis, up_basis, head_group):
    tok, feat = hidden_rows.shape
    n = lax.axis_size("dp")
    part = feat // n
    piece = WIDTH // min(n, WIDTH // 16)
    chunks = max(feat, n * tok) // CHUNK
    heads = jnp.arange(HEADS, dtype=jnp.int32)
    same = head_group[:, None] == head_group[None, :]
    before = jnp.sum((same & (heads[None, :] < heads[:, None])).astype(jnp.int32), axis=1)
    place = head_group * PER + before
    order = jnp.sum(jnp.where(place[None, :] == heads[:, None], heads[None, :], 0), axis=1)
    vmem = pl.BlockSpec(memory_space=pltpu.VMEM)
    dma = pltpu.SemaphoreType.DMA
    qs = pl.pallas_call(
        sort_heads,
        out_shape=jax.ShapeDtypeStruct((HEADS * tok, HD), BF16),
        in_specs=[pl.BlockSpec(memory_space=pltpu.SMEM), vmem],
        out_specs=vmem,
    )(order, queries)
    rows, up, err = pl.pallas_call(
        functools.partial(kernel, n, tok, feat),
        out_shape=(
            jax.ShapeDtypeStruct((part, WIDTH), BF16),
            jax.ShapeDtypeStruct((WIDTH, HD), BF16),
            jax.ShapeDtypeStruct((tok, 1), F32),
        ),
        in_specs=[vmem] * 5,
        out_specs=(vmem, vmem, vmem),
        scratch_shapes=[
            pltpu.VMEM((feat, tok), BF16),
            pltpu.VMEM((part, n * tok), BF16),
            pltpu.VMEM((tok, WIDTH), BF16),
            pltpu.VMEM((n * tok, WIDTH), BF16),
            pltpu.VMEM((n * tok, WIDTH), BF16),
            pltpu.VMEM((feat, WIDTH), BF16),
            pltpu.VMEM((WIDTH, HD), BF16),
            pltpu.VMEM((WIDTH, HD), BF16),
            pltpu.VMEM((WIDTH, HD), BF16),
            pltpu.VMEM((WIDTH, HD), BF16),
            pltpu.VMEM((2, n, piece, HD), BF16),
            pltpu.VMEM((2, n, piece, HD), BF16),
            pltpu.VMEM((4, n, piece, HD), BF16),
            pltpu.VMEM((4, WIDTH, HD), BF16),
            dma, dma,
            dma((4,)), dma((4,)), dma((4,)), dma((4,)),
            dma((3, chunks // 2)), dma((3,)), dma((3,)), dma((3,)), dma((3, chunks // 2)),
        ],
        compiler_params=pltpu.CompilerParams(
            collective_id=0, has_side_effects=True, vmem_limit_bytes=48 * 1024 * 1024
        ),
    )(hidden_rows, qs, keys, down_basis, up_basis.reshape(WIDTH, HD))
    return rows, up.reshape(GROUPS, HD, HD), err.reshape(tok)


def solution(mesh):
    return jax.shard_map(
        shards,
        mesh=mesh,
        in_specs=(
            P(("parts", "dp"), None),
            P(("parts", "dp"), None),
            P(("parts", "dp"), None),
            P("parts", None),
            P("parts", None, None),
            P(),
        ),
        out_specs=(P(("parts", "dp"), None), P("parts", None, None), P(("parts", "dp"))),
        check_vma=False,
    )
```
